32 devices in a mesh: zonal: 8 (over z, x), merid: 4 (over y, core).
Axes of the slice: x: 2, y: 2, z: 4, core: 2. Of those that a mesh axis runs over, the one named last changes fastest.
Arguments:
- field: bfloat16 [64, 512, 256], P('merid', 'zonal'), may hold values from -6 to 6
- weight_one: bfloat16 [3, 3, 256, 256], replicated, may hold values from -0.125 to 0.125
- bias_one: float32 [256], replicated, may hold values from -3 to 3
- weight_two: bfloat16 [3, 3, 256, 256], replicated, may hold values from -0.125 to 0.125
- bias_two: float32 [256], replicated, may hold values from -3 to 3
- depth_levels: int32 [64, 512], P('merid', 'zonal'), may hold values from 0 to 64
- fold_partner: int32 [512], replicated, may hold values from 0 to 511, as said below
- cotangent: bfloat16 [64, 512, 256], P('merid', 'zonal'), may hold values from -6 to 6
Outputs:
- output: bfloat16 [64, 512, 256], P('merid', 'zonal')
- input_grad: bfloat16 [64, 512, 256], P('merid', 'zonal')
- grad_one: float32 [3, 3, 256, 256], replicated
- grad_two: float32 [3, 3, 256, 256], replicated
The draws below stay inside these ranges and needn't reach their ends.
Inputs may be any that keep to these rules, and one draw needn't show every extreme that they name: fold_partner[i] = (511 - i + s) mod 512 with one pivot offset s, 0 to 511, for the whole table.
All inputs are finite; a program needn't handle non-finite values.
Results may differ from the reference program's by a relative error of at most 0.003.
Values may be sent and summed in bfloat16 or wider, within the bound.
A program may use at most 128 MiB of HBM per device.

```python
import math
from functools import partial
import jax
import jax.numpy as jnp
from jax import lax

C = 256
LEV = 64
NY = 64
NX = 512


def draw_fold_partner(key, part):
    offset = jax.random.randint(key, (), 0, NX, dtype=jnp.int32)
    index = jnp.arange(NX, dtype=jnp.int32)
    return (NX - 1 - index + offset) % NX


def touch_ends(values, own_key, smallest, largest):
    extent = values.shape
    spot = [jax.random.randint(jax.random.fold_in(own_key, axis), (), 0, extent[axis]) for axis in range(len(extent))]
    values = values.at[tuple(spot)].set(smallest)
    longest = extent.index(max(extent))
    spot[longest] = (spot[longest] + 1) % extent[longest]
    return values.at[tuple(spot)].set(largest)


def steps_of(rng, shape, split, smallest, top_value):
    loudness = 1.0
    for dim, parts in split:
        heights = jax.random.uniform(jax.random.fold_in(jax.random.fold_in(rng, 6), dim), (parts,), jnp.float32, smallest / len(split), top_value / len(split))
        loudness = loudness * jnp.repeat(jnp.exp(heights), shape[dim] // parts).reshape((-1,) + (1,) * (len(shape) - 1 - dim))
    return loudness


def bell_draw(key, extent, width, limit, pieces=(), held_as=jnp.bfloat16):
    array = width * jax.random.normal(key, extent, jnp.float32)
    if pieces:
        array = array * steps_of(key, extent, pieces, -0.22, 0.18)
    return jnp.clip(array, -limit, limit).astype(held_as)


def setup_inputs(seed: int = 0) -> dict:
    key_of = jax.random.split(jax.random.key(seed), 9)
    field = bell_draw(key_of[0], (NY, NX, C), 1.0, 6.0, ((0, 4), (1, 8)))
    weight_one = bell_draw(key_of[1], (3, 3, C, C), (9 * C) ** -0.5, 0.125)
    bias_one = bell_draw(key_of[2], (C,), 0.5, 3.0, (), jnp.float32)
    weight_two = bell_draw(key_of[3], (3, 3, C, C), (9 * C) ** -0.5, 0.125)
    bias_two = bell_draw(key_of[4], (C,), 0.5, 3.0, (), jnp.float32)
    depth_levels = touch_ends(jax.random.randint(key_of[5], (NY, NX), 0, LEV + 1), jax.random.fold_in(key_of[5], 1), 0, LEV).astype(jnp.int32)
    fold_partner = draw_fold_partner(jax.random.fold_in(key_of[8], 71), 0)
    cotangent = bell_draw(key_of[7], (NY, NX, C), 1.0, 6.0, ((0, 4), (1, 8)))
    return {"field": field, "weight_one": weight_one, "bias_one": bias_one, "weight_two": weight_two, "bias_two": bias_two, "depth_levels": depth_levels, "fold_partner": fold_partner, "cotangent": cotangent}


def pad_whole(values, fold_partner):
    fold_row = jnp.take(values[-1], fold_partner, axis=0)
    with_rows = jnp.concatenate([jnp.zeros_like(values[:1]), values, fold_row[None]], axis=0)
    return jnp.concatenate([with_rows[:, -1:], with_rows, with_rows[:, :1]], axis=1)

def convolve(padded, weight):
    result = jnp.zeros((NY, NX, weight.shape[3]), padded.dtype)
    for row_step in range(3):
        for col_step in range(3):
            window = padded[row_step:row_step + NY, col_step:col_step + NX]
            result = result + jnp.einsum('yxc,cd->yxd', window, weight[row_step, col_step], precision=lax.Precision.HIGHEST)
    return result

def reference(field, weight_one, bias_one, weight_two, bias_two, depth_levels, fold_partner, cotangent):
    level_index = jnp.arange(C, dtype=jnp.int32) % LEV
    mask = (level_index[None, None, :] < depth_levels[:, :, None]).astype(jnp.float32)
    field_pad = pad_whole(field, fold_partner).astype(jnp.float32)
    pre_one, back_one = jax.vjp(convolve, field_pad, weight_one.astype(jnp.float32))
    pre_one = pre_one + bias_one
    hidden = lax.optimization_barrier((jax.nn.gelu(pre_one) * mask).astype(jnp.bfloat16))
    hidden_pad = pad_whole(hidden, fold_partner).astype(jnp.float32)
    pre_two, back_two = jax.vjp(convolve, hidden_pad, weight_two.astype(jnp.float32))
    output = ((field.astype(jnp.float32) + pre_two + bias_two) * mask).astype(jnp.bfloat16)
    masked_grad = cotangent.astype(jnp.float32) * mask
    delta_two = lax.optimization_barrier(masked_grad.astype(jnp.bfloat16)).astype(jnp.float32)
    hidden_pad_grad, weight_two_grad = back_two(delta_two)
    _, pad_back = jax.vjp(partial(pad_whole, fold_partner=fold_partner), jnp.zeros((NY, NX, C), jnp.float32))
    hidden_grad = pad_back(hidden_pad_grad)[0]
    _, gelu_back = jax.vjp(jax.nn.gelu, pre_one)
    delta_one = gelu_back(hidden_grad * mask)[0]
    delta_one = lax.optimization_barrier(delta_one.astype(jnp.bfloat16)).astype(jnp.float32)
    field_pad_grad, weight_one_grad = back_one(delta_one)
    input_grad = (masked_grad + pad_back(field_pad_grad)[0]).astype(jnp.bfloat16)
    scale = 1.0 / math.sqrt(NY * NX)
    return (output, input_grad, weight_one_grad * scale, weight_two_grad * scale)
```

```python
import functools
import math

import jax
import jax.numpy as jnp
from jax import lax
from jax.experimental import pallas as pl
from jax.experimental.pallas import tpu as pltpu
from jax.sharding import PartitionSpec as P

LEV = 64
MESH = pl.DeviceIdType.MESH
BF = jnp.bfloat16
F32 = jnp.float32
GELU_A = math.sqrt(2.0 / math.pi)
GELU_B = 0.044715


def plan_steps(total, nz, nm):
    merid_bits = [("merid", 1 << i) for i in range(nm.bit_length() - 1)]
    zonal_bits = [("zonal", 1 << i) for i in range(nz.bit_length() - 1)]
    order_one = merid_bits + zonal_bits
    order_two = merid_bits[:1] + zonal_bits[1:2] + merid_bits[1:] + zonal_bits[:1] + zonal_bits[2:]
    plans = []
    for order in (order_one, order_two):
        size, plan = total, []
        for step, (axis, bit) in enumerate(order):
            halve = size % 32 == 0
            if halve:
                size //= 2
            plan.append((axis, bit, size, halve, step == 0 or step > 2))
        plans.append(plan)
    return plans


def kernel(
    nz, nm, rows, cols, plans,
    field, delta_in, mask, w_one, b_one, w_two, b_two, partner_tab,
    out, in_grad, sums,
    va, vb, gp, hg,
    q_field, q_hidden, q_two, q_one, ql_two, ql_one, wt_one, wt_two, wl_one, wl_two,
    west, east, north, south, cols32,
    row_send, col_send, row_recv, col_recv, fold_all, acc, ar_send, ar_recv, ar_wide,
    halo_ss, halo_rs, fold_ss, fold_rs, ar_ss, ar_rs, ag_ss, ag_rs,
):
    ch = field.shape[1]
    cells = rows * cols
    z = lax.axis_index("zonal")
    m = lax.axis_index("merid")
    zw = (z + nz - 1) % nz
    ze = (z + 1) % nz
    has_n = m < nm - 1
    has_s = m > 0
    is_top = m == nm - 1

    def partner_of(axis, bit):
        index = z if axis == "zonal" else m
        mine = (index // bit) % 2
        other = index + bit - 2 * bit * mine
        if axis == "zonal":
            return mine, {"zonal": other, "merid": m}
        return mine, {"zonal": z, "merid": other}

    barrier = pltpu.get_barrier_semaphore()

    def greet(mm, zz):
        pl.semaphore_signal(
            barrier, 1, device_id={"zonal": zz, "merid": mm}, device_id_type=MESH
        )

    greet(m, zw)
    greet(m, ze)
    for axis, bit, _, _, _ in plans[0]:
        _, other = partner_of(axis, bit)
        greet(other["merid"], other["zonal"])

    @pl.when(has_n)
    def _():
        for zz in (zw, z, ze):
            greet(m + 1, zz)

    @pl.when(has_s)
    def _():
        for zz in (zw, z, ze):
            greet(m - 1, zz)

    @pl.when(is_top)
    def _():
        @pl.loop(1, nz)
        def _(k):
            greet(m, (z + k) % nz)

    def copy_to(src, dst, ssem, rsem, mm, zz):
        return pltpu.make_async_remote_copy(
            src_ref=src, dst_ref=dst, send_sem=ssem, recv_sem=rsem,
            device_id={"zonal": zz, "merid": mm}, device_id_type=MESH,
        )

    def col_copy(p, slot, mm, zz):
        src = col_send.at[p, 0 if slot < 3 else 1]
        return copy_to(src, col_recv.at[p, slot], halo_ss.at[p, slot], halo_rs.at[p, slot], mm, zz)

    def row_copy(p, slot, mm, zz):
        return copy_to(
            row_send.at[p, slot], row_recv.at[p, slot],
            halo_ss.at[p, 6 + slot], halo_rs.at[p, 6 + slot], mm, zz,
        )

    def fold_copy(p, source, target):
        return copy_to(
            row_send.at[p, 0], fold_all.at[p, source],
            fold_ss.at[p, target], fold_rs.at[p, source], m, target,
        )

    def prepare(p):
        for k, v in enumerate((va, vb)):
            row_send[p, 0, k * cols:(k + 1) * cols, :] = v[cells - cols:, :].astype(BF)
            row_send[p, 1, k * cols:(k + 1) * cols, :] = v[:cols, :].astype(BF)
            for side, x in ((0, cols - 1), (1, 0)):
                for y in range(rows):
                    cols32[y:y + 1, :] = v[y * cols + x:y * cols + x + 1, :]
                col_send[p, side, k * rows:(k + 1) * rows, :] = cols32[...].astype(BF)

    def halo(p, what):
        def act(copy):
            getattr(copy, what)()

        act(col_copy(p, 0, m, ze))
        act(col_copy(p, 3, m, zw))

        @pl.when(has_n)
        def _():
            act(row_copy(p, 0, m + 1, z))
            act(col_copy(p, 1, m + 1, ze))
            act(col_copy(p, 4, m + 1, zw))

        @pl.when(has_s)
        def _():
            act(row_copy(p, 1, m - 1, z))
            act(col_copy(p, 2, m - 1, ze))
            act(col_copy(p, 5, m - 1, zw))

        @pl.when(is_top)
        def _():
            @pl.loop(1, nz)
            def _(k):
                act(fold_copy(p, z, (z + k) % nz))

    def halo_arrive(p):
        col_copy(p, 0, m, ze).wait_recv()
        col_copy(p, 3, m, zw).wait_recv()

        @pl.when(has_s)
        def _():
            row_copy(p, 0, m, ze).wait_recv()
            col_copy(p, 1, m, ze).wait_recv()
            col_copy(p, 4, m, zw).wait_recv()

        @pl.when(has_n)
        def _():
            row_copy(p, 1, m, ze).wait_recv()
            col_copy(p, 2, m, ze).wait_recv()
            col_copy(p, 5, m, zw).wait_recv()

        @pl.when(is_top)
        def _():
            fold_all[p, z, :, :] = row_send[p, 0, :, :]

            @pl.loop(1, nz)
            def _(k):
                fold_copy(p, (z + nz - k) % nz, ze).wait_recv()

    spot = lax.broadcasted_iota(jnp.int32, (cols, ch), 0)

    def emit(row, wrow, erow, q, off):
        left = jnp.where(spot == 0, wrow, pltpu.roll(row, 1, 0))
        right = jnp.where(spot == cols - 1, erow, pltpu.roll(row, cols - 1, 0))
        q[pl.ds(off, cols), 0:ch] = left.astype(BF)
        q[pl.ds(off, cols), ch:2 * ch] = row.astype(BF)
        q[pl.ds(off, cols), 2 * ch:3 * ch] = right.astype(BF)

    def assemble(p, k, v, q, ql):
        mine = slice(k * rows, (k + 1) * rows)
        span = slice(k * cols, (k + 1) * cols)
        west[0:rows, :] = col_recv[p, 0, mine, :].astype(F32)
        east[0:rows, :] = col_recv[p, 3, mine, :].astype(F32)

        @pl.when(has_s)
        def _():
            south[...] = row_recv[p, 0, span, :].astype(F32)
            west[rows:rows + 1, :] = col_recv[p, 1, mine, :].astype(F32)[rows - 1:rows, :]
            east[rows:rows + 1, :] = col_recv[p, 4, mine, :].astype(F32)[rows - 1:rows, :]

        @pl.when(jnp.logical_not(has_s))
        def _():
            south[...] = jnp.zeros_like(south)
            west[rows:rows + 1, :] = jnp.zeros((1, ch), F32)
            east[rows:rows + 1, :] = jnp.zeros((1, ch), F32)

        @pl.when(has_n)
        def _():
            north[...] = row_recv[p, 1, span, :].astype(F32)
            west[rows + 1:rows + 2, :] = col_recv[p, 2, mine, :].astype(F32)[0:1, :]
            east[rows + 1:rows + 2, :] = col_recv[p, 5, mine, :].astype(F32)[0:1, :]

        @pl.when(is_top)
        def _():
            around = nz * cols
            extra = cols + 16
            first = partner_tab[0]
            at = lax.broadcasted_iota(jnp.int32, (extra, around), 0)
            column = z * cols + jnp.where(at < cols, at, jnp.where(at == cols, -1, cols))
            target = first - column
            target = jnp.where(target < 0, target + around, target)
            target = jnp.where(target >= around, target - around, target)
            source = lax.broadcasted_iota(jnp.int32, (extra, around), 1)
            pick = jnp.where(target == source, 1.0, 0.0).astype(BF)
            whole_row = fold_all[p, :, span, :].reshape(around, ch)
            folded = jnp.dot(pick, whole_row, preferred_element_type=F32)
            north[...] = folded[0:cols, :]
            west[rows + 1:rows + 2, :] = folded[cols:cols + 1, :]
            east[rows + 1:rows + 2, :] = folded[cols + 1:cols + 2, :]

        @pl.loop(0, rows)
        def _(y):
            off = pl.multiple_of(y * cols, cols)
            emit(
                v[pl.ds(off, cols), :], west[pl.ds(y, 1), :], east[pl.ds(y, 1), :],
                q, pl.multiple_of(off + cols, cols),
            )

        emit(south[...], west[rows:rows + 1, :], east[rows:rows + 1, :], q, 0)
        if ql is None:
            emit(north[...], west[rows + 1:rows + 2, :], east[rows + 1:rows + 2, :], q, cells + cols)
        else:
            emit(north[...], west[rows + 1:rows + 2, :], east[rows + 1:rows + 2, :], ql, 0)
            q[cells + cols:, :] = jnp.zeros((cols, 3 * ch), BF)

    chunk = 4 * cols

    def conv(q, w, finish):
        @pl.loop(0, cells // chunk)
        def _(i):
            off = pl.multiple_of(i * chunk, chunk)
            total = jnp.dot(q[pl.ds(off, chunk), :], w[0], preferred_element_type=F32)
            for a in (1, 2):
                at = pl.multiple_of(off + a * cols, cols)
                total += jnp.dot(q[pl.ds(at, chunk), :], w[a], preferred_element_type=F32)
            finish(pl.ds(off, chunk), total)

    def transpose_weights(w, wt, wl):
        @pl.loop(0, 3)
        def _(a):
            for b in range(3):
                turned = w[2 - a, (2 - b) * ch:(3 - b) * ch, :].astype(F32).T
                wt[a, b * ch:(b + 1) * ch, :] = turned.astype(BF)

        for b in range(3):
            @pl.when(is_top)
            def _():
                wl[b * ch:(b + 1) * ch, :] = wt[0, (2 - b) * ch:(3 - b) * ch, :]

            @pl.when(jnp.logical_not(is_top))
            def _():
                wl[b * ch:(b + 1) * ch, :] = wt[2, b * ch:(b + 1) * ch, :]

    def last_row(ql, wl, target):
        target[cells - cols:, :] += jnp.dot(ql[...], wl[...], preferred_element_type=F32)

    def gradient(g, q, e_turned):
        for a in range(3):
            for b in range(3):
                part = jnp.dot(
                    e_turned, q[a * cols:a * cols + cells, b * ch:(b + 1) * ch],
                    preferred_element_type=F32,
                )
                acc[g, (3 * a + b) * ch:(3 * a + b + 1) * ch, :] = part.T

    def loop_rows(count, body):
        piece = 48 if count % 48 == 0 else 16

        @pl.loop(0, count // piece)
        def _(i):
            body(i * piece, piece)

    def reduce_all(g):
        low = 0
        place = 0
        place_wide = 0
        waits = []
        gathers = []
        for step, (axis, bit, size, halve, wide) in enumerate(plans[g]):
            mine, other = partner_of(axis, bit)
            keep = low + mine * size if halve else low
            give = low + (1 - mine) * size if halve else low
            if halve:
                gathers.append((step, axis, bit, size, low))

            def fill(off, piece, give=give, place=place):
                ar_send[g, pl.ds(place + pl.multiple_of(off, 16), piece), :] = acc[
                    g, pl.ds(pl.multiple_of(give + off, 16), piece), :
                ].astype(BF)

            if wide:
                source = acc.at[g, pl.ds(pl.multiple_of(give, 16), size)]
                landing, start = ar_wide, place_wide
                place_wide += size
            else:
                loop_rows(size, fill)
                source = ar_send.at[g, pl.ds(place, size)]
                landing, start = ar_recv, place
            copy = copy_to(
                source, landing.at[g, pl.ds(start, size)],
                ar_ss.at[g, step], ar_rs.at[g, step], other["merid"], other["zonal"],
            )
            copy.start()
            yield
            copy.wait_recv()
            if wide and not halve:
                copy.wait_send()
            else:
                waits.append(copy)

            def add(
                off, piece, keep=keep, place=place, rounded=not (halve or wide),
                landing=landing, start=start,
            ):
                at = pl.ds(pl.multiple_of(keep + off, 16), piece)
                here = pl.ds(start + pl.multiple_of(off, 16), piece)
                own = ar_send[g, here, :].astype(F32) if rounded else acc[g, at, :]
                acc[g, at, :] = own + landing[g, here, :].astype(F32)

            loop_rows(size, add)
            if not wide:
                place += size
            low = keep
        final = plans[g][-1][2]

        def settle(off, piece, low=low):
            at = pl.ds(pl.multiple_of(low + off, 16), piece)
            sums[g, at, :] = acc[g, at, :].astype(BF)

        loop_rows(final, settle)
        size = final
        for step, axis, bit, size, base in reversed(gathers):
            mine, other = partner_of(axis, bit)
            at = pl.ds(pl.multiple_of(base + mine * size, 16), size)
            theirs = pl.ds(pl.multiple_of(base + (1 - mine) * size, 16), size)
            copy = copy_to(
                sums.at[g, at], sums.at[g, at], ag_ss.at[g, step], ag_rs.at[g, step],
                other["merid"], other["zonal"],
            )
            copy.start()
            waits.append(copy)
            yield
            copy_to(
                sums.at[g, theirs], sums.at[g, theirs], ag_ss.at[g, step], ag_rs.at[g, step],
                other["merid"], other["zonal"],
            ).wait_recv()
        for copy in waits:
            copy.wait_send()

    va[...] = field[...].astype(F32)
    vb[...] = delta_in[...].astype(F32)
    prepare(0)
    count = (
        2 + len(plans[0]) + jnp.where(has_n, 3, 0) + jnp.where(has_s, 3, 0)
        + jnp.where(is_top, nz - 1, 0)
    )
    pl.semaphore_wait(barrier, count)
    halo(0, "start")
    transpose_weights(w_two, wt_two, wl_two)
    transpose_weights(w_one, wt_one, wl_one)
    halo_arrive(0)
    assemble(0, 0, va, q_field, None)
    assemble(0, 1, vb, q_two, ql_two)

    def finish_one(at, total):
        x = total + b_one[...]
        keep = mask[at, :].astype(F32)
        square = x * x
        t = jnp.tanh(GELU_A * x * (1.0 + GELU_B * square))
        half = 0.5 * (1.0 + t)
        va[at, :] = (x * half * keep).astype(BF).astype(F32)
        slope = half + 0.5 * x * (1.0 - t * t) * (GELU_A * (1.0 + 3.0 * GELU_B * square))
        gp[at, :] = slope * keep

    conv(q_field, w_one, finish_one)

    def finish_hg(at, total):
        hg[at, :] = total

    conv(q_two, wt_two, finish_hg)
    last_row(ql_two, wl_two, hg)

    @pl.loop(0, rows)
    def _(y):
        at = pl.ds(pl.multiple_of(y * cols, cols), cols)
        vb[at, :] = (gp[at, :] * hg[at, :]).astype(BF).astype(F32)

    prepare(1)
    halo(1, "start")

    gradient(0, q_field, vb[...].T.astype(BF))
    first = reduce_all(0)
    next(first)
    halo_arrive(1)
    assemble(1, 0, va, q_hidden, None)
    assemble(1, 1, vb, q_one, ql_one)
    next(first)
    gradient(1, q_hidden, delta_in[...].astype(F32).T.astype(BF))
    second = reduce_all(1)
    next(second)

    def advance(gen):
        return next(gen, "end") != "end"

    advance(first)
    advance(second)

    def finish_out(at, total):
        full = field[at, :].astype(F32) + total + b_two[...]
        out[at, :] = (full * mask[at, :].astype(F32)).astype(BF)

    conv(q_hidden, w_two, finish_out)
    advance(first)
    advance(second)
    conv(q_one, wt_one, finish_hg)
    last_row(ql_one, wl_one, hg)

    @pl.loop(0, rows)
    def _(y):
        at = pl.ds(pl.multiple_of(y * cols, cols), cols)
        in_grad[at, :] = (delta_in[at, :].astype(F32) + hg[at, :]).astype(BF)

    more = True
    while more:
        one = advance(first)
        two = advance(second)
        more = one or two
    halo(0, "wait_send")
    halo(1, "wait_send")


def shards(
    field, weight_one, bias_one, weight_two, bias_two, depth_levels, fold_partner, cotangent,
    nz, nm,
):
    rows, cols, ch = field.shape
    cells = rows * cols
    total = 9 * ch
    level = lax.broadcasted_iota(jnp.int32, (1, 1, ch), 2) % LEV
    mask = (level < depth_levels[:, :, None]).astype(BF)
    delta = cotangent * mask
    plans = plan_steps(total, nz, nm)
    sent = max(sum(step[2] for step in plan if not step[4]) for plan in plans)
    sent_wide = max(sum(step[2] for step in plan if step[4]) for plan in plans)
    steps = len(plans[0])
    vmem = pl.BlockSpec(memory_space=pltpu.VMEM)
    smem = pl.BlockSpec(memory_space=pltpu.SMEM)
    wide = 3 * ch
    dma = pltpu.SemaphoreType.DMA
    out, in_grad, sums = pl.pallas_call(
        functools.partial(kernel, nz, nm, rows, cols, plans),
        out_shape=(
            jax.ShapeDtypeStruct((cells, ch), BF),
            jax.ShapeDtypeStruct((cells, ch), BF),
            jax.ShapeDtypeStruct((2, total, ch), BF),
        ),
        in_specs=[vmem] * 7 + [smem],
        out_specs=(vmem, vmem, vmem),
        scratch_shapes=[
            pltpu.VMEM((cells, ch), F32), pltpu.VMEM((cells, ch), F32),
            pltpu.VMEM((cells, ch), F32), pltpu.VMEM((cells, ch), F32),
            pltpu.VMEM((cells + 2 * cols, wide), BF), pltpu.VMEM((cells + 2 * cols, wide), BF),
            pltpu.VMEM((cells + 2 * cols, wide), BF), pltpu.VMEM((cells + 2 * cols, wide), BF),
            pltpu.VMEM((cols, wide), BF), pltpu.VMEM((cols, wide), BF),
            pltpu.VMEM((3, wide, ch), BF), pltpu.VMEM((3, wide, ch), BF),
            pltpu.VMEM((wide, ch), BF), pltpu.VMEM((wide, ch), BF),
            pltpu.VMEM((rows + 8, ch), F32), pltpu.VMEM((rows + 8, ch), F32),
            pltpu.VMEM((cols, ch), F32), pltpu.VMEM((cols, ch), F32),
            pltpu.VMEM((rows, ch), F32),
            pltpu.VMEM((2, 2, 2 * cols, ch), BF), pltpu.VMEM((2, 2, 2 * rows, ch), BF),
            pltpu.VMEM((2, 2, 2 * cols, ch), BF), pltpu.VMEM((2, 6, 2 * rows, ch), BF),
            pltpu.VMEM((2, nz, 2 * cols, ch), BF),
            pltpu.VMEM((2, total, ch), F32),
            pltpu.VMEM((2, sent, ch), BF), pltpu.VMEM((2, sent, ch), BF),
            pltpu.VMEM((2, sent_wide, ch), F32),
            dma((2, 8)), dma((2, 8)), dma((2, nz)), dma((2, nz)),
            dma((2, steps)), dma((2, steps)), dma((2, steps)), dma((2, steps)),
        ],
        compiler_params=pltpu.CompilerParams(
            collective_id=0, has_side_effects=True, vmem_limit_bytes=58 * 1024 * 1024
        ),
    )(
        field.reshape(cells, ch), delta.reshape(cells, ch), mask.reshape(cells, ch),
        weight_one.reshape(3, wide, ch), bias_one.reshape(1, ch),
        weight_two.reshape(3, wide, ch), bias_two.reshape(1, ch), fold_partner,
    )
    scale = 1.0 / math.sqrt(cells * nz * nm)
    grads = sums.astype(F32) * scale
    shape = weight_one.shape
    return (
        out.reshape(field.shape), in_grad.reshape(field.shape),
        grads[0].reshape(shape), grads[1].reshape(shape),
    )


def solution(mesh):
    placed = (
        P("merid", "zonal", None), P(), P(), P(), P(), P("merid", "zonal"), P(),
        P("merid", "zonal", None),
    )
    return jax.shard_map(
        functools.partial(shards, nz=mesh.shape["zonal"], nm=mesh.shape["merid"]),
        mesh=mesh,
        in_specs=placed,
        out_specs=(P("merid", "zonal", None), P("merid", "zonal", None), P(), P()),
        check_vma=False,
    )
```

```python
import functools
import math

import jax
import jax.numpy as jnp
from jax import lax
from jax.experimental import pallas as pl
from jax.experimental.pallas import tpu as pltpu
from jax.sharding import PartitionSpec as P

LEV = 64
MESH = pl.DeviceIdType.MESH
BF = jnp.bfloat16
F32 = jnp.float32
GELU_A = math.sqrt(2.0 / math.pi)
GELU_B = 0.044715


def plan_steps(total, nz, nm):
    merid_bits = [("merid", 1 << i) for i in range(nm.bit_length() - 1)]
    zonal_bits = [("zonal", 1 << i) for i in range(nz.bit_length() - 1)]
    rest = merid_bits[1:] + zonal_bits
    plans = []
    for turn in range(3):
        order = merid_bits[:1] + rest[turn:3] + rest[:turn] + rest[3:]
        size, plan = total // 3, []
        for step, (axis, bit) in enumerate(order):
            halve = size % 32 == 0
            if halve:
                size //= 2
            plan.append((axis, bit, size, halve, step == 0 or step > 2))
        plans.append(plan)
    return plans


def kernel(
    nz, nm, rows, cols, plans,
    field, delta_in, mask, w_one, b_one, w_two, b_two, partner_tab,
    out, in_grad, sums,
    va, vb, gp, hg,
    q_field, q_hidden, q_two, q_one, ql_two, ql_one, wt_one, wt_two, wl_one, wl_two,
    west, east, north, south, cols32,
    row_send, col_send, row_recv, col_recv, fold_all, acc, ar_send, ar_recv, ar_wide,
    halo_ss, halo_rs, fold_ss, fold_rs, ar_ss, ar_rs, ag_ss, ag_rs,
):
    ch = field.shape[1]
    cells = rows * cols
    z = lax.axis_index("zonal")
    m = lax.axis_index("merid")
    zw = (z + nz - 1) % nz
    ze = (z + 1) % nz
    has_n = m < nm - 1
    has_s = m > 0
    is_top = m == nm - 1

    def partner_of(axis, bit):
        index = z if axis == "zonal" else m
        mine = (index // bit) % 2
        other = index + bit - 2 * bit * mine
        if axis == "zonal":
            return mine, {"zonal": other, "merid": m}
        return mine, {"zonal": z, "merid": other}

    barrier = pltpu.get_barrier_semaphore()

    def greet(mm, zz):
        pl.semaphore_signal(
            barrier, 1, device_id={"zonal": zz, "merid": mm}, device_id_type=MESH
        )

    greet(m, zw)
    greet(m, ze)
    for axis, bit, _, _, _ in plans[0]:
        _, other = partner_of(axis, bit)
        greet(other["merid"], other["zonal"])

    @pl.when(has_n)
    def _():
        for zz in (zw, z, ze):
            greet(m + 1, zz)

    @pl.when(has_s)
    def _():
        for zz in (zw, z, ze):
            greet(m - 1, zz)

    @pl.when(is_top)
    def _():
        @pl.loop(1, nz)
        def _(k):
            greet(m, (z + k) % nz)

    def copy_to(src, dst, ssem, rsem, mm, zz):
        return pltpu.make_async_remote_copy(
            src_ref=src, dst_ref=dst, send_sem=ssem, recv_sem=rsem,
            device_id={"zonal": zz, "merid": mm}, device_id_type=MESH,
        )

    def col_copy(p, slot, mm, zz):
        src = col_send.at[p, 0 if slot < 3 else 1]
        return copy_to(src, col_recv.at[p, slot], halo_ss.at[p, slot], halo_rs.at[p, slot], mm, zz)

    def row_copy(p, slot, mm, zz):
        return copy_to(
            row_send.at[p, slot], row_recv.at[p, slot],
            halo_ss.at[p, 6 + slot], halo_rs.at[p, 6 + slot], mm, zz,
        )

    def fold_copy(p, source, target):
        return copy_to(
            row_send.at[p, 0], fold_all.at[p, source],
            fold_ss.at[p, target], fold_rs.at[p, source], m, target,
        )

    def prepare(p):
        for k, v in enumerate((va, vb)):
            row_send[p, 0, k * cols:(k + 1) * cols, :] = v[cells - cols:, :].astype(BF)
            row_send[p, 1, k * cols:(k + 1) * cols, :] = v[:cols, :].astype(BF)
            for side, x in ((0, cols - 1), (1, 0)):
                for y in range(rows):
                    cols32[y:y + 1, :] = v[y * cols + x:y * cols + x + 1, :]
                col_send[p, side, k * rows:(k + 1) * rows, :] = cols32[...].astype(BF)

    def halo(p, what):
        def act(copy):
            getattr(copy, what)()

        act(col_copy(p, 0, m, ze))
        act(col_copy(p, 3, m, zw))

        @pl.when(has_n)
        def _():
            act(row_copy(p, 0, m + 1, z))
            act(col_copy(p, 1, m + 1, ze))
            act(col_copy(p, 4, m + 1, zw))

        @pl.when(has_s)
        def _():
            act(row_copy(p, 1, m - 1, z))
            act(col_copy(p, 2, m - 1, ze))
            act(col_copy(p, 5, m - 1, zw))

        @pl.when(is_top)
        def _():
            @pl.loop(1, nz)
            def _(k):
                act(fold_copy(p, z, (z + k) % nz))

    def halo_arrive(p):
        col_copy(p, 0, m, ze).wait_recv()
        col_copy(p, 3, m, zw).wait_recv()

        @pl.when(has_s)
        def _():
            row_copy(p, 0, m, ze).wait_recv()
            col_copy(p, 1, m, ze).wait_recv()
            col_copy(p, 4, m, zw).wait_recv()

        @pl.when(has_n)
        def _():
            row_copy(p, 1, m, ze).wait_recv()
            col_copy(p, 2, m, ze).wait_recv()
            col_copy(p, 5, m, zw).wait_recv()

        @pl.when(is_top)
        def _():
            fold_all[p, z, :, :] = row_send[p, 0, :, :]

            @pl.loop(1, nz)
            def _(k):
                fold_copy(p, (z + nz - k) % nz, ze).wait_recv()

    spot = lax.broadcasted_iota(jnp.int32, (cols, ch), 0)

    def emit(row, wrow, erow, q, off):
        left = jnp.where(spot == 0, wrow, pltpu.roll(row, 1, 0))
        right = jnp.where(spot == cols - 1, erow, pltpu.roll(row, cols - 1, 0))
        q[pl.ds(off, cols), 0:ch] = left.astype(BF)
        q[pl.ds(off, cols), ch:2 * ch] = row.astype(BF)
        q[pl.ds(off, cols), 2 * ch:3 * ch] = right.astype(BF)

    def assemble(p, k, v, q, ql):
        mine = slice(k * rows, (k + 1) * rows)
        span = slice(k * cols, (k + 1) * cols)
        west[0:rows, :] = col_recv[p, 0, mine, :].astype(F32)
        east[0:rows, :] = col_recv[p, 3, mine, :].astype(F32)

        @pl.when(has_s)
        def _():
            south[...] = row_recv[p, 0, span, :].astype(F32)
            west[rows:rows + 1, :] = col_recv[p, 1, mine, :].astype(F32)[rows - 1:rows, :]
            east[rows:rows + 1, :] = col_recv[p, 4, mine, :].astype(F32)[rows - 1:rows, :]

        @pl.when(jnp.logical_not(has_s))
        def _():
            south[...] = jnp.zeros_like(south)
            west[rows:rows + 1, :] = jnp.zeros((1, ch), F32)
            east[rows:rows + 1, :] = jnp.zeros((1, ch), F32)

        @pl.when(has_n)
        def _():
            north[...] = row_recv[p, 1, span, :].astype(F32)
            west[rows + 1:rows + 2, :] = col_recv[p, 2, mine, :].astype(F32)[0:1, :]
            east[rows + 1:rows + 2, :] = col_recv[p, 5, mine, :].astype(F32)[0:1, :]

        @pl.when(is_top)
        def _():
            around = nz * cols
            extra = cols + 16
            first = partner_tab[0]
            at = lax.broadcasted_iota(jnp.int32, (extra, around), 0)
            column = z * cols + jnp.where(at < cols, at, jnp.where(at == cols, -1, cols))
            target = first - column
            target = jnp.where(target < 0, target + around, target)
            target = jnp.where(target >= around, target - around, target)
            source = lax.broadcasted_iota(jnp.int32, (extra, around), 1)
            pick = jnp.where(target == source, 1.0, 0.0).astype(BF)
            whole_row = fold_all[p, :, span, :].reshape(around, ch)
            folded = jnp.dot(pick, whole_row, preferred_element_type=F32)
            north[...] = folded[0:cols, :]
            west[rows + 1:rows + 2, :] = folded[cols:cols + 1, :]
            east[rows + 1:rows + 2, :] = folded[cols + 1:cols + 2, :]

        @pl.loop(0, rows)
        def _(y):
            off = pl.multiple_of(y * cols, cols)
            emit(
                v[pl.ds(off, cols), :], west[pl.ds(y, 1), :], east[pl.ds(y, 1), :],
                q, pl.multiple_of(off + cols, cols),
            )

        emit(south[...], west[rows:rows + 1, :], east[rows:rows + 1, :], q, 0)
        if ql is None:
            emit(north[...], west[rows + 1:rows + 2, :], east[rows + 1:rows + 2, :], q, cells + cols)
        else:
            emit(north[...], west[rows + 1:rows + 2, :], east[rows + 1:rows + 2, :], ql, 0)
            q[cells + cols:, :] = jnp.zeros((cols, 3 * ch), BF)

    chunk = 4 * cols

    def conv(q, w, finish):
        @pl.loop(0, cells // chunk)
        def _(i):
            off = pl.multiple_of(i * chunk, chunk)
            total = jnp.dot(q[pl.ds(off, chunk), :], w[0], preferred_element_type=F32)
            for a in (1, 2):
                at = pl.multiple_of(off + a * cols, cols)
                total += jnp.dot(q[pl.ds(at, chunk), :], w[a], preferred_element_type=F32)
            finish(pl.ds(off, chunk), total)

    def transpose_weights(w, wt, wl):
        @pl.loop(0, 3)
        def _(a):
            for b in range(3):
                turned = w[2 - a, (2 - b) * ch:(3 - b) * ch, :].astype(F32).T
                wt[a, b * ch:(b + 1) * ch, :] = turned.astype(BF)

        for b in range(3):
            @pl.when(is_top)
            def _():
                wl[b * ch:(b + 1) * ch, :] = wt[0, (2 - b) * ch:(3 - b) * ch, :]

            @pl.when(jnp.logical_not(is_top))
            def _():
                wl[b * ch:(b + 1) * ch, :] = wt[2, b * ch:(b + 1) * ch, :]

    def last_row(ql, wl, target):
        target[cells - cols:, :] += jnp.dot(ql[...], wl[...], preferred_element_type=F32)

    def gradient(g, a, q, e_turned):
        for b in range(3):
            part = jnp.dot(
                e_turned, q[a * cols:a * cols + cells, b * ch:(b + 1) * ch],
                preferred_element_type=F32,
            )
            acc[g, (3 * a + b) * ch:(3 * a + b + 1) * ch, :] = part.T

    def loop_rows(count, body):
        piece = 48 if count % 48 == 0 else 16

        @pl.loop(0, count // piece)
        def _(i):
            body(i * piece, piece)

    def reduce_all(g, a):
        lane = 3 * g + a
        plan = plans[a]
        low = 3 * a * ch
        place = 0
        place_wide = 0
        waits = []
        gathers = []
        for step, (axis, bit, size, halve, wide) in enumerate(plan):
            mine, other = partner_of(axis, bit)
            keep = low + mine * size if halve else low
            give = low + (1 - mine) * size if halve else low
            if halve:
                gathers.append((step, axis, bit, size, low))

            def fill(off, piece, give=give, place=place):
                ar_send[lane, pl.ds(place + pl.multiple_of(off, 16), piece), :] = acc[
                    g, pl.ds(pl.multiple_of(give + off, 16), piece), :
                ].astype(BF)

            if wide:
                source = acc.at[g, pl.ds(pl.multiple_of(give, 16), size)]
                landing, start = ar_wide, place_wide
                place_wide += size
            else:
                loop_rows(size, fill)
                source = ar_send.at[lane, pl.ds(place, size)]
                landing, start = ar_recv, place
            copy = copy_to(
                source, landing.at[lane, pl.ds(start, size)],
                ar_ss.at[lane, step], ar_rs.at[lane, step], other["merid"], other["zonal"],
            )
            copy.start()
            yield
            copy.wait_recv()
            if wide and not halve:
                copy.wait_send()
            else:
                waits.append(copy)

            def add(
                off, piece, keep=keep, place=place, rounded=not (halve or wide),
                landing=landing, start=start,
            ):
                at = pl.ds(pl.multiple_of(keep + off, 16), piece)
                here = pl.ds(start + pl.multiple_of(off, 16), piece)
                own = ar_send[lane, here, :].astype(F32) if rounded else acc[g, at, :]
                acc[g, at, :] = own + landing[lane, here, :].astype(F32)

            loop_rows(size, add)
            if not wide:
                place += size
            low = keep
        final = plan[-1][2]

        def settle(off, piece, low=low):
            at = pl.ds(pl.multiple_of(low + off, 16), piece)
            sums[g, at, :] = acc[g, at, :].astype(BF)

        loop_rows(final, settle)
        size = final
        for step, axis, bit, size, base in reversed(gathers):
            mine, other = partner_of(axis, bit)
            at = pl.ds(pl.multiple_of(base + mine * size, 16), size)
            theirs = pl.ds(pl.multiple_of(base + (1 - mine) * size, 16), size)
            copy = copy_to(
                sums.at[g, at], sums.at[g, at], ag_ss.at[lane, step], ag_rs.at[lane, step],
                other["merid"], other["zonal"],
            )
            copy.start()
            waits.append(copy)
            yield
            copy_to(
                sums.at[g, theirs], sums.at[g, theirs], ag_ss.at[lane, step], ag_rs.at[lane, step],
                other["merid"], other["zonal"],
            ).wait_recv()
        for copy in waits:
            copy.wait_send()

    va[...] = field[...].astype(F32)
    vb[...] = delta_in[...].astype(F32)
    prepare(0)
    count = (
        2 + len(plans[0]) + jnp.where(has_n, 3, 0) + jnp.where(has_s, 3, 0)
        + jnp.where(is_top, nz - 1, 0)
    )
    pl.semaphore_wait(barrier, count)
    halo(0, "start")
    transpose_weights(w_two, wt_two, wl_two)
    transpose_weights(w_one, wt_one, wl_one)
    halo_arrive(0)
    assemble(0, 0, va, q_field, None)
    assemble(0, 1, vb, q_two, ql_two)

    def finish_one(at, total):
        x = total + b_one[...]
        keep = mask[at, :].astype(F32)
        square = x * x
        t = jnp.tanh(GELU_A * x * (1.0 + GELU_B * square))
        half = 0.5 * (1.0 + t)
        va[at, :] = (x * half * keep).astype(BF).astype(F32)
        slope = half + 0.5 * x * (1.0 - t * t) * (GELU_A * (1.0 + 3.0 * GELU_B * square))
        gp[at, :] = slope * keep

    conv(q_field, w_one, finish_one)

    def finish_hg(at, total):
        hg[at, :] = total

    conv(q_two, wt_two, finish_hg)
    last_row(ql_two, wl_two, hg)

    @pl.loop(0, rows)
    def _(y):
        at = pl.ds(pl.multiple_of(y * cols, cols), cols)
        vb[at, :] = (gp[at, :] * hg[at, :]).astype(BF).astype(F32)

    prepare(1)
    halo(1, "start")

    chains = []

    def advance():
        going = [next(chain, "end") != "end" for chain in chains]
        return any(going)

    def begin(g, a, q, e_turned):
        gradient(g, a, q, e_turned)
        chain = reduce_all(g, a)
        next(chain)
        chains.append(chain)

    turned = vb[...].T.astype(BF)
    for a in range(3):
        begin(0, a, q_field, turned)
    halo_arrive(1)
    assemble(1, 0, va, q_hidden, None)
    advance()
    turned = delta_in[...].astype(F32).T.astype(BF)
    for a in range(3):
        begin(1, a, q_hidden, turned)
    advance()

    assemble(1, 1, vb, q_one, ql_one)
    advance()

    def finish_out(at, total):
        full = field[at, :].astype(F32) + total + b_two[...]
        out[at, :] = (full * mask[at, :].astype(F32)).astype(BF)

    conv(q_hidden, w_two, finish_out)
    advance()
    conv(q_one, wt_one, finish_hg)
    last_row(ql_one, wl_one, hg)
    advance()

    @pl.loop(0, rows)
    def _(y):
        at = pl.ds(pl.multiple_of(y * cols, cols), cols)
        in_grad[at, :] = (delta_in[at, :].astype(F32) + hg[at, :]).astype(BF)

    while advance():
        pass
    halo(0, "wait_send")
    halo(1, "wait_send")


def shards(
    field, weight_one, bias_one, weight_two, bias_two, depth_levels, fold_partner, cotangent,
    nz, nm,
):
    rows, cols, ch = field.shape
    cells = rows * cols
    total = 9 * ch
    level = lax.broadcasted_iota(jnp.int32, (1, 1, ch), 2) % LEV
    mask = (level < depth_levels[:, :, None]).astype(BF)
    delta = cotangent * mask
    plans = plan_steps(total, nz, nm)
    sent = max(sum(step[2] for step in plan if not step[4]) for plan in plans)
    sent_wide = max(sum(step[2] for step in plan if step[4]) for plan in plans)
    steps = len(plans[0])
    vmem = pl.BlockSpec(memory_space=pltpu.VMEM)
    smem = pl.BlockSpec(memory_space=pltpu.SMEM)
    wide = 3 * ch
    dma = pltpu.SemaphoreType.DMA
    out, in_grad, sums = pl.pallas_call(
        functools.partial(kernel, nz, nm, rows, cols, plans),
        out_shape=(
            jax.ShapeDtypeStruct((cells, ch), BF),
            jax.ShapeDtypeStruct((cells, ch), BF),
            jax.ShapeDtypeStruct((2, total, ch), BF),
        ),
        in_specs=[vmem] * 7 + [smem],
        out_specs=(vmem, vmem, vmem),
        scratch_shapes=[
            pltpu.VMEM((cells, ch), F32), pltpu.VMEM((cells, ch), F32),
            pltpu.VMEM((cells, ch), F32), pltpu.VMEM((cells, ch), F32),
            pltpu.VMEM((cells + 2 * cols, wide), BF), pltpu.VMEM((cells + 2 * cols, wide), BF),
            pltpu.VMEM((cells + 2 * cols, wide), BF), pltpu.VMEM((cells + 2 * cols, wide), BF),
            pltpu.VMEM((cols, wide), BF), pltpu.VMEM((cols, wide), BF),
            pltpu.VMEM((3, wide, ch), BF), pltpu.VMEM((3, wide, ch), BF),
            pltpu.VMEM((wide, ch), BF), pltpu.VMEM((wide, ch), BF),
            pltpu.VMEM((rows + 8, ch), F32), pltpu.VMEM((rows + 8, ch), F32),
            pltpu.VMEM((cols, ch), F32), pltpu.VMEM((cols, ch), F32),
            pltpu.VMEM((rows, ch), F32),
            pltpu.VMEM((2, 2, 2 * cols, ch), BF), pltpu.VMEM((2, 2, 2 * rows, ch), BF),
            pltpu.VMEM((2, 2, 2 * cols, ch), BF), pltpu.VMEM((2, 6, 2 * rows, ch), BF),
            pltpu.VMEM((2, nz, 2 * cols, ch), BF),
            pltpu.VMEM((2, total, ch), F32),
            pltpu.VMEM((6, sent, ch), BF), pltpu.VMEM((6, sent, ch), BF),
            pltpu.VMEM((6, sent_wide, ch), F32),
            dma((2, 8)), dma((2, 8)), dma((2, nz)), dma((2, nz)),
            dma((6, steps)), dma((6, steps)), dma((6, steps)), dma((6, steps)),
        ],
        compiler_params=pltpu.CompilerParams(
            collective_id=0, has_side_effects=True, vmem_limit_bytes=58 * 1024 * 1024
        ),
    )(
        field.reshape(cells, ch), delta.reshape(cells, ch), mask.reshape(cells, ch),
        weight_one.reshape(3, wide, ch), bias_one.reshape(1, ch),
        weight_two.reshape(3, wide, ch), bias_two.reshape(1, ch), fold_partner,
    )
    scale = 1.0 / math.sqrt(cells * nz * nm)
    grads = sums.astype(F32) * scale
    shape = weight_one.shape
    return (
        out.reshape(field.shape), in_grad.reshape(field.shape),
        grads[0].reshape(shape), grads[1].reshape(shape),
    )


def solution(mesh):
    placed = (
        P("merid", "zonal", None), P(), P(), P(), P(), P("merid", "zonal"), P(),
        P("merid", "zonal", None),
    )
    return jax.shard_map(
        functools.partial(shards, nz=mesh.shape["zonal"], nm=mesh.shape["merid"]),
        mesh=mesh,
        in_specs=placed,
        out_specs=(P("merid", "zonal", None), P("merid", "zonal", None), P(), P()),
        check_vma=False,
    )
```

```python
import functools
import math

import jax
import jax.numpy as jnp
from jax import lax
from jax.experimental import pallas as pl
from jax.experimental.pallas import tpu as pltpu
from jax.sharding import PartitionSpec as P

LEV = 64
MESH = pl.DeviceIdType.MESH
BF = jnp.bfloat16
F32 = jnp.float32
GELU_A = math.sqrt(2.0 / math.pi)
GELU_B = 0.044715


def plan_steps(total, nz, nm):
    merid_bits = [("merid", 1 << i) for i in range(nm.bit_length() - 1)]
    zonal_bits = [("zonal", 1 << i) for i in range(nz.bit_length() - 1)]
    rest = merid_bits[1:] + zonal_bits
    plans = []
    for turn in range(3):
        order = merid_bits[:1] + rest[turn:3] + rest[:turn] + rest[3:]
        size, plan = total // 3, []
        for step, (axis, bit) in enumerate(order):
            halve = size % 32 == 0
            if halve:
                size //= 2
            plan.append((axis, bit, size, halve, step == 0 or step > 2))
        plans.append(plan)
    return plans


def kernel(
    nz, nm, rows, cols, plans,
    field, cotangent, depth, w_one, b_one, w_two, b_two, partner_tab,
    out, in_grad, sums,
    va, vb, gp, hg, mask, delta_in,
    q_field, q_hidden, q_two, q_one, ql_two, ql_one, wt_one, wt_two, wl_one, wl_two,
    west, east, north, south, cols32,
    row_send, col_send, row_recv, col_recv, fold_all, acc, ar_send, ar_recv, ar_wide,
    halo_ss, halo_rs, fold_ss, fold_rs, ar_ss, ar_rs, ag_ss, ag_rs,
):
    ch = field.shape[1]
    cells = rows * cols
    z = lax.axis_index("zonal")
    m = lax.axis_index("merid")
    zw = (z + nz - 1) % nz
    ze = (z + 1) % nz
    has_n = m < nm - 1
    has_s = m > 0
    is_top = m == nm - 1

    def partner_of(axis, bit):
        index = z if axis == "zonal" else m
        mine = (index // bit) % 2
        other = index + bit - 2 * bit * mine
        if axis == "zonal":
            return mine, {"zonal": other, "merid": m}
        return mine, {"zonal": z, "merid": other}

    barrier = pltpu.get_barrier_semaphore()

    def greet(mm, zz):
        pl.semaphore_signal(
            barrier, 1, device_id={"zonal": zz, "merid": mm}, device_id_type=MESH
        )

    greet(m, zw)
    greet(m, ze)
    for axis, bit, _, _, _ in plans[0]:
        _, other = partner_of(axis, bit)
        greet(other["merid"], other["zonal"])

    @pl.when(has_n)
    def _():
        for zz in (zw, z, ze):
            greet(m + 1, zz)

    @pl.when(has_s)
    def _():
        for zz in (zw, z, ze):
            greet(m - 1, zz)

    @pl.when(is_top)
    def _():
        @pl.loop(1, nz)
        def _(k):
            greet(m, (z + k) % nz)

    def copy_to(src, dst, ssem, rsem, mm, zz):
        return pltpu.make_async_remote_copy(
            src_ref=src, dst_ref=dst, send_sem=ssem, recv_sem=rsem,
            device_id={"zonal": zz, "merid": mm}, device_id_type=MESH,
        )

    def col_copy(p, slot, mm, zz):
        src = col_send.at[p, 0 if slot < 3 else 1]
        return copy_to(src, col_recv.at[p, slot], halo_ss.at[p, slot], halo_rs.at[p, slot], mm, zz)

    def row_copy(p, slot, mm, zz):
        return copy_to(
            row_send.at[p, slot], row_recv.at[p, slot],
            halo_ss.at[p, 6 + slot], halo_rs.at[p, 6 + slot], mm, zz,
        )

    def fold_copy(p, source, target):
        return copy_to(
            row_send.at[p, 0], fold_all.at[p, source],
            fold_ss.at[p, target], fold_rs.at[p, source], m, target,
        )

    def prepare(p):
        for k, v in enumerate((va, vb)):
            row_send[p, 0, k * cols:(k + 1) * cols, :] = v[cells - cols:, :].astype(BF)
            row_send[p, 1, k * cols:(k + 1) * cols, :] = v[:cols, :].astype(BF)
            for side, x in ((0, cols - 1), (1, 0)):
                for y in range(rows):
                    cols32[y:y + 1, :] = v[y * cols + x:y * cols + x + 1, :]
                col_send[p, side, k * rows:(k + 1) * rows, :] = cols32[...].astype(BF)

    def halo(p, what):
        def act(copy):
            getattr(copy, what)()

        act(col_copy(p, 0, m, ze))
        act(col_copy(p, 3, m, zw))

        @pl.when(has_n)
        def _():
            act(row_copy(p, 0, m + 1, z))
            act(col_copy(p, 1, m + 1, ze))
            act(col_copy(p, 4, m + 1, zw))

        @pl.when(has_s)
        def _():
            act(row_copy(p, 1, m - 1, z))
            act(col_copy(p, 2, m - 1, ze))
            act(col_copy(p, 5, m - 1, zw))

        @pl.when(is_top)
        def _():
            @pl.loop(1, nz)
            def _(k):
                act(fold_copy(p, z, (z + k) % nz))

    def halo_arrive(p):
        col_copy(p, 0, m, ze).wait_recv()
        col_copy(p, 3, m, zw).wait_recv()

        @pl.when(has_s)
        def _():
            row_copy(p, 0, m, ze).wait_recv()
            col_copy(p, 1, m, ze).wait_recv()
            col_copy(p, 4, m, zw).wait_recv()

        @pl.when(has_n)
        def _():
            row_copy(p, 1, m, ze).wait_recv()
            col_copy(p, 2, m, ze).wait_recv()
            col_copy(p, 5, m, zw).wait_recv()

        @pl.when(is_top)
        def _():
            fold_all[p, z, :, :] = row_send[p, 0, :, :]

            @pl.loop(1, nz)
            def _(k):
                fold_copy(p, (z + nz - k) % nz, ze).wait_recv()

    spot = lax.broadcasted_iota(jnp.int32, (cols, ch), 0)

    def emit(row, wrow, erow, q, off):
        left = jnp.where(spot == 0, wrow, pltpu.roll(row, 1, 0))
        right = jnp.where(spot == cols - 1, erow, pltpu.roll(row, cols - 1, 0))
        q[pl.ds(off, cols), 0:ch] = left.astype(BF)
        q[pl.ds(off, cols), ch:2 * ch] = row.astype(BF)
        q[pl.ds(off, cols), 2 * ch:3 * ch] = right.astype(BF)

    def assemble(p, k, v, q, ql):
        mine = slice(k * rows, (k + 1) * rows)
        span = slice(k * cols, (k + 1) * cols)
        west[0:rows, :] = col_recv[p, 0, mine, :].astype(F32)
        east[0:rows, :] = col_recv[p, 3, mine, :].astype(F32)

        @pl.when(has_s)
        def _():
            south[...] = row_recv[p, 0, span, :].astype(F32)
            west[rows:rows + 1, :] = col_recv[p, 1, mine, :].astype(F32)[rows - 1:rows, :]
            east[rows:rows + 1, :] = col_recv[p, 4, mine, :].astype(F32)[rows - 1:rows, :]

        @pl.when(jnp.logical_not(has_s))
        def _():
            south[...] = jnp.zeros_like(south)
            west[rows:rows + 1, :] = jnp.zeros((1, ch), F32)
            east[rows:rows + 1, :] = jnp.zeros((1, ch), F32)

        @pl.when(has_n)
        def _():
            north[...] = row_recv[p, 1, span, :].astype(F32)
            west[rows + 1:rows + 2, :] = col_recv[p, 2, mine, :].astype(F32)[0:1, :]
            east[rows + 1:rows + 2, :] = col_recv[p, 5, mine, :].astype(F32)[0:1, :]

        @pl.when(is_top)
        def _():
            around = nz * cols
            extra = cols + 16
            first = partner_tab[0]
            at = lax.broadcasted_iota(jnp.int32, (extra, around), 0)
            column = z * cols + jnp.where(at < cols, at, jnp.where(at == cols, -1, cols))
            target = first - column
            target = jnp.where(target < 0, target + around, target)
            target = jnp.where(target >= around, target - around, target)
            source = lax.broadcasted_iota(jnp.int32, (extra, around), 1)
            pick = jnp.where(target == source, 1.0, 0.0).astype(BF)
            whole_row = fold_all[p, :, span, :].reshape(around, ch)
            folded = jnp.dot(pick, whole_row, preferred_element_type=F32)
            north[...] = folded[0:cols, :]
            west[rows + 1:rows + 2, :] = folded[cols:cols + 1, :]
            east[rows + 1:rows + 2, :] = folded[cols + 1:cols + 2, :]

        @pl.loop(0, rows, unroll=2)
        def _(y):
            off = pl.multiple_of(y * cols, cols)
            emit(
                v[pl.ds(off, cols), :], west[pl.ds(y, 1), :], east[pl.ds(y, 1), :],
                q, pl.multiple_of(off + cols, cols),
            )

        emit(south[...], west[rows:rows + 1, :], east[rows:rows + 1, :], q, 0)
        if ql is None:
            emit(north[...], west[rows + 1:rows + 2, :], east[rows + 1:rows + 2, :], q, cells + cols)
        else:
            emit(north[...], west[rows + 1:rows + 2, :], east[rows + 1:rows + 2, :], ql, 0)
            q[cells + cols:, :] = jnp.zeros((cols, 3 * ch), BF)

    chunk = 4 * cols

    def conv(q, w, finish):
        @pl.loop(0, cells // chunk)
        def _(i):
            off = pl.multiple_of(i * chunk, chunk)
            total = jnp.dot(q[pl.ds(off, chunk), :], w[0], preferred_element_type=F32)
            for a in (1, 2):
                at = pl.multiple_of(off + a * cols, cols)
                total += jnp.dot(q[pl.ds(at, chunk), :], w[a], preferred_element_type=F32)
            finish(pl.ds(off, chunk), total)

    def transpose_weights(w, wt, wl):
        @pl.loop(0, 3)
        def _(a):
            for b in range(3):
                turned = w[2 - a, (2 - b) * ch:(3 - b) * ch, :].astype(F32).T
                wt[a, b * ch:(b + 1) * ch, :] = turned.astype(BF)

        for b in range(3):
            @pl.when(is_top)
            def _():
                wl[b * ch:(b + 1) * ch, :] = wt[0, (2 - b) * ch:(3 - b) * ch, :]

            @pl.when(jnp.logical_not(is_top))
            def _():
                wl[b * ch:(b + 1) * ch, :] = wt[2, b * ch:(b + 1) * ch, :]

    def last_row(ql, wl, target):
        target[cells - cols:, :] += jnp.dot(ql[...], wl[...], preferred_element_type=F32)

    def gradient(g, a, q, e_turned):
        for b in range(3):
            part = jnp.dot(
                e_turned, q[a * cols:a * cols + cells, b * ch:(b + 1) * ch],
                preferred_element_type=F32,
            )
            acc[g, (3 * a + b) * ch:(3 * a + b + 1) * ch, :] = part.T

    def loop_rows(count, body):
        piece = next(size for size in (192, 96, 48, 16) if count % size == 0)

        @pl.loop(0, count // piece)
        def _(i):
            body(i * piece, piece)

    def reduce_all(g, a):
        lane = 3 * g + a
        plan = plans[a]
        low = 3 * a * ch
        place = 0
        place_wide = 0
        waits = []
        gathers = []
        for step, (axis, bit, size, halve, wide) in enumerate(plan):
            mine, other = partner_of(axis, bit)
            keep = low + mine * size if halve else low
            give = low + (1 - mine) * size if halve else low
            if halve:
                gathers.append((step, axis, bit, size, low))

            def fill(off, piece, give=give, place=place):
                ar_send[lane, pl.ds(place + pl.multiple_of(off, 16), piece), :] = acc[
                    g, pl.ds(pl.multiple_of(give + off, 16), piece), :
                ].astype(BF)

            if wide:
                source = acc.at[g, pl.ds(pl.multiple_of(give, 16), size)]
                landing, start = ar_wide, place_wide
                place_wide += size
            else:
                loop_rows(size, fill)
                source = ar_send.at[lane, pl.ds(place, size)]
                landing, start = ar_recv, place
            copy = copy_to(
                source, landing.at[lane, pl.ds(start, size)],
                ar_ss.at[lane, step], ar_rs.at[lane, step], other["merid"], other["zonal"],
            )
            copy.start()
            yield
            copy.wait_recv()
            if wide and not halve:
                copy.wait_send()
            else:
                waits.append(copy)

            def add(
                off, piece, keep=keep, place=place, rounded=not (halve or wide),
                landing=landing, start=start,
            ):
                at = pl.ds(pl.multiple_of(keep + off, 16), piece)
                here = pl.ds(start + pl.multiple_of(off, 16), piece)
                own = ar_send[lane, here, :].astype(F32) if rounded else acc[g, at, :]
                acc[g, at, :] = own + landing[lane, here, :].astype(F32)

            loop_rows(size, add)
            if not wide:
                place += size
            low = keep
        final = plan[-1][2]

        def settle(off, piece, low=low):
            at = pl.ds(pl.multiple_of(low + off, 16), piece)
            sums[g, at, :] = acc[g, at, :].astype(BF)

        loop_rows(final, settle)
        size = final
        for step, axis, bit, size, base in reversed(gathers):
            mine, other = partner_of(axis, bit)
            at = pl.ds(pl.multiple_of(base + mine * size, 16), size)
            theirs = pl.ds(pl.multiple_of(base + (1 - mine) * size, 16), size)
            copy = copy_to(
                sums.at[g, at], sums.at[g, at], ag_ss.at[lane, step], ag_rs.at[lane, step],
                other["merid"], other["zonal"],
            )
            copy.start()
            waits.append(copy)
            yield
            copy_to(
                sums.at[g, theirs], sums.at[g, theirs], ag_ss.at[lane, step], ag_rs.at[lane, step],
                other["merid"], other["zonal"],
            ).wait_recv()
        for copy in waits:
            copy.wait_send()

    va[...] = field[...].astype(F32)
    channel = lax.broadcasted_iota(jnp.int32, (cols, ch), 1)
    level = channel
    for first in range(LEV, ch, LEV):
        level = level - jnp.where(channel >= first, LEV, 0)
    for y in range(rows):
        at = slice(y * cols, (y + 1) * cols)
        wet = jnp.where(level < depth[:, y:y + 1], 1.0, 0.0)
        masked = cotangent[at, :].astype(F32) * wet
        mask[at, :] = wet
        vb[at, :] = masked
        delta_in[at, :] = masked.astype(BF)
    prepare(0)
    count = (
        2 + len(plans[0]) + jnp.where(has_n, 3, 0) + jnp.where(has_s, 3, 0)
        + jnp.where(is_top, nz - 1, 0)
    )
    pl.semaphore_wait(barrier, count)
    halo(0, "start")
    transpose_weights(w_two, wt_two, wl_two)
    transpose_weights(w_one, wt_one, wl_one)
    halo_arrive(0)
    assemble(0, 0, va, q_field, None)
    assemble(0, 1, vb, q_two, ql_two)

    def finish_one(at, total):
        x = total + b_one[...]
        keep = mask[at, :]
        square = x * x
        t = jnp.tanh(GELU_A * x * (1.0 + GELU_B * square))
        half = 0.5 * (1.0 + t)
        va[at, :] = (x * half * keep).astype(BF).astype(F32)
        slope = half + 0.5 * x * (1.0 - t * t) * (GELU_A * (1.0 + 3.0 * GELU_B * square))
        gp[at, :] = slope * keep

    conv(q_field, w_one, finish_one)

    def finish_hg(at, total):
        hg[at, :] = total

    conv(q_two, wt_two, finish_hg)
    last_row(ql_two, wl_two, hg)

    @pl.loop(0, rows)
    def _(y):
        at = pl.ds(pl.multiple_of(y * cols, cols), cols)
        vb[at, :] = (gp[at, :] * hg[at, :]).astype(BF).astype(F32)

    prepare(1)
    halo(1, "start")

    chains = []

    def advance():
        going = [next(chain, "end") != "end" for chain in chains]
        return any(going)

    def begin(g, a, q, e_turned):
        gradient(g, a, q, e_turned)
        chain = reduce_all(g, a)
        next(chain)
        chains.append(chain)

    turned = vb[...].T.astype(BF)
    for a in range(3):
        begin(0, a, q_field, turned)
    halo_arrive(1)
    assemble(1, 0, va, q_hidden, None)
    advance()
    turned = delta_in[...].astype(F32).T.astype(BF)
    for a in range(3):
        begin(1, a, q_hidden, turned)
    advance()

    assemble(1, 1, vb, q_one, ql_one)
    advance()

    def finish_out(at, total):
        full = field[at, :].astype(F32) + total + b_two[...]
        out[at, :] = (full * mask[at, :]).astype(BF)

    conv(q_hidden, w_two, finish_out)
    advance()
    conv(q_one, wt_one, finish_hg)
    last_row(ql_one, wl_one, hg)
    advance()

    @pl.loop(0, rows)
    def _(y):
        at = pl.ds(pl.multiple_of(y * cols, cols), cols)
        in_grad[at, :] = (delta_in[at, :].astype(F32) + hg[at, :]).astype(BF)

    while advance():
        pass
    halo(0, "wait_send")
    halo(1, "wait_send")


def shards(
    field, weight_one, bias_one, weight_two, bias_two, depth_levels, fold_partner, cotangent,
    nz, nm,
):
    rows, cols, ch = field.shape
    cells = rows * cols
    total = 9 * ch
    plans = plan_steps(total, nz, nm)
    sent = max(sum(step[2] for step in plan if not step[4]) for plan in plans)
    sent_wide = max(sum(step[2] for step in plan if step[4]) for plan in plans)
    steps = len(plans[0])
    vmem = pl.BlockSpec(memory_space=pltpu.VMEM)
    smem = pl.BlockSpec(memory_space=pltpu.SMEM)
    wide = 3 * ch
    dma = pltpu.SemaphoreType.DMA
    out, in_grad, sums = pl.pallas_call(
        functools.partial(kernel, nz, nm, rows, cols, plans),
        out_shape=(
            jax.ShapeDtypeStruct((cells, ch), BF),
            jax.ShapeDtypeStruct((cells, ch), BF),
            jax.ShapeDtypeStruct((2, total, ch), BF),
        ),
        in_specs=[vmem] * 7 + [smem],
        out_specs=(vmem, vmem, vmem),
        scratch_shapes=[
            pltpu.VMEM((cells, ch), F32), pltpu.VMEM((cells, ch), F32),
            pltpu.VMEM((cells, ch), F32), pltpu.VMEM((cells, ch), F32),
            pltpu.VMEM((cells, ch), F32), pltpu.VMEM((cells, ch), BF),
            pltpu.VMEM((cells + 2 * cols, wide), BF), pltpu.VMEM((cells + 2 * cols, wide), BF),
            pltpu.VMEM((cells + 2 * cols, wide), BF), pltpu.VMEM((cells + 2 * cols, wide), BF),
            pltpu.VMEM((cols, wide), BF), pltpu.VMEM((cols, wide), BF),
            pltpu.VMEM((3, wide, ch), BF), pltpu.VMEM((3, wide, ch), BF),
            pltpu.VMEM((wide, ch), BF), pltpu.VMEM((wide, ch), BF),
            pltpu.VMEM((rows + 8, ch), F32), pltpu.VMEM((rows + 8, ch), F32),
            pltpu.VMEM((cols, ch), F32), pltpu.VMEM((cols, ch), F32),
            pltpu.VMEM((rows, ch), F32),
            pltpu.VMEM((2, 2, 2 * cols, ch), BF), pltpu.VMEM((2, 2, 2 * rows, ch), BF),
            pltpu.VMEM((2, 2, 2 * cols, ch), BF), pltpu.VMEM((2, 6, 2 * rows, ch), BF),
            pltpu.VMEM((2, nz, 2 * cols, ch), BF),
            pltpu.VMEM((2, total, ch), F32),
            pltpu.VMEM((6, sent, ch), BF), pltpu.VMEM((6, sent, ch), BF),
            pltpu.VMEM((6, sent_wide, ch), F32),
            dma((2, 8)), dma((2, 8)), dma((2, nz)), dma((2, nz)),
            dma((6, steps)), dma((6, steps)), dma((6, steps)), dma((6, steps)),
        ],
        compiler_params=pltpu.CompilerParams(
            collective_id=0, has_side_effects=True, vmem_limit_bytes=58 * 1024 * 1024
        ),
    )(
        field.reshape(cells, ch), cotangent.reshape(cells, ch), depth_levels.T,
        weight_one.reshape(3, wide, ch), bias_one.reshape(1, ch),
        weight_two.reshape(3, wide, ch), bias_two.reshape(1, ch), fold_partner,
    )
    scale = 1.0 / math.sqrt(cells * nz * nm)
    grads = sums.astype(F32) * scale
    shape = weight_one.shape
    return (
        out.reshape(field.shape), in_grad.reshape(field.shape),
        grads[0].reshape(shape), grads[1].reshape(shape),
    )


def solution(mesh):
    placed = (
        P("merid", "zonal", None), P(), P(), P(), P(), P("merid", "zonal"), P(),
        P("merid", "zonal", None),
    )
    return jax.shard_map(
        functools.partial(shards, nz=mesh.shape["zonal"], nm=mesh.shape["merid"]),
        mesh=mesh,
        in_specs=placed,
        out_specs=(P("merid", "zonal", None), P("merid", "zonal", None), P(), P()),
        check_vma=False,
    )
```

```python
import functools
import math

import jax
import jax.numpy as jnp
from jax import lax
from jax.experimental import pallas as pl
from jax.experimental.pallas import tpu as pltpu
from jax.sharding import PartitionSpec as P

LEV = 64
MESH = pl.DeviceIdType.MESH
BF = jnp.bfloat16
F32 = jnp.float32
GELU_A = math.sqrt(2.0 / math.pi)
GELU_B = 0.044715


def plan_steps(total, nz, nm):
    merid_bits = [("merid", 1 << i) for i in range(nm.bit_length() - 1)]
    zonal_bits = [("zonal", 1 << i) for i in range(nz.bit_length() - 1)]
    rest = merid_bits[1:] + zonal_bits
    plans = []
    for turn in range(3):
        order = merid_bits[:1] + rest[turn:3] + rest[:turn] + rest[3:]
        size, plan = total // 3, []
        for step, (axis, bit) in enumerate(order):
            halve = size % 32 == 0
            if halve:
                size //= 2
            plan.append((axis, bit, size, halve, step == 0 or step > 2))
        plans.append(plan)
    return plans


def kernel(
    nz, nm, rows, cols, plans,
    field, cotangent, depth, w_one, b_one, w_two, b_two, partner_tab,
    out, in_grad, sums,
    va, vb, gp, hg, mask, delta_in,
    q_field, q_hidden, q_two, q_one, ql_two, ql_one, wt_one, wt_two, wl_one, wl_two,
    west, east, north, south, cols32,
    row_send, col_send, row_recv, col_recv, fold_all, acc, ar_send, ar_recv, ar_wide,
    halo_ss, halo_rs, fold_ss, fold_rs, ar_ss, ar_rs, ag_ss, ag_rs,
):
    ch = field.shape[1]
    cells = rows * cols
    z = lax.axis_index("zonal")
    m = lax.axis_index("merid")
    zw = (z + nz - 1) % nz
    ze = (z + 1) % nz
    has_n = m < nm - 1
    has_s = m > 0
    is_top = m == nm - 1

    def partner_of(axis, bit):
        index = z if axis == "zonal" else m
        mine = (index // bit) % 2
        other = index + bit - 2 * bit * mine
        if axis == "zonal":
            return mine, {"zonal": other, "merid": m}
        return mine, {"zonal": z, "merid": other}

    barrier = pltpu.get_barrier_semaphore()

    def greet(mm, zz):
        pl.semaphore_signal(
            barrier, 1, device_id={"zonal": zz, "merid": mm}, device_id_type=MESH
        )

    greet(m, zw)
    greet(m, ze)
    for axis, bit, _, _, _ in plans[0]:
        _, other = partner_of(axis, bit)
        greet(other["merid"], other["zonal"])

    @pl.when(has_n)
    def _():
        for zz in (zw, z, ze):
            greet(m + 1, zz)

    @pl.when(has_s)
    def _():
        for zz in (zw, z, ze):
            greet(m - 1, zz)

    @pl.when(is_top)
    def _():
        @pl.loop(1, nz)
        def _(k):
            greet(m, (z + k) % nz)

    def copy_to(src, dst, ssem, rsem, mm, zz):
        return pltpu.make_async_remote_copy(
            src_ref=src, dst_ref=dst, send_sem=ssem, recv_sem=rsem,
            device_id={"zonal": zz, "merid": mm}, device_id_type=MESH,
        )

    def col_copy(p, slot, mm, zz):
        src = col_send.at[p, 0 if slot < 3 else 1]
        return copy_to(src, col_recv.at[p, slot], halo_ss.at[p, slot], halo_rs.at[p, slot], mm, zz)

    def row_copy(p, slot, mm, zz):
        return copy_to(
            row_send.at[p, slot], row_recv.at[p, slot],
            halo_ss.at[p, 6 + slot], halo_rs.at[p, 6 + slot], mm, zz,
        )

    def fold_copy(p, source, target):
        return copy_to(
            row_send.at[p, 0], fold_all.at[p, source],
            fold_ss.at[p, target], fold_rs.at[p, source], m, target,
        )

    def prepare(p):
        for k, v in enumerate((va, vb)):
            row_send[p, 0, k * cols:(k + 1) * cols, :] = v[cells - cols:, :].astype(BF)
            row_send[p, 1, k * cols:(k + 1) * cols, :] = v[:cols, :].astype(BF)
            for side, x in ((0, cols - 1), (1, 0)):
                for y in range(rows):
                    cols32[y:y + 1, :] = v[y * cols + x:y * cols + x + 1, :]
                col_send[p, side, k * rows:(k + 1) * rows, :] = cols32[...].astype(BF)

    def halo(p, what):
        def act(copy):
            getattr(copy, what)()

        act(col_copy(p, 0, m, ze))
        act(col_copy(p, 3, m, zw))

        @pl.when(has_n)
        def _():
            act(row_copy(p, 0, m + 1, z))
            act(col_copy(p, 1, m + 1, ze))
            act(col_copy(p, 4, m + 1, zw))

        @pl.when(has_s)
        def _():
            act(row_copy(p, 1, m - 1, z))
            act(col_copy(p, 2, m - 1, ze))
            act(col_copy(p, 5, m - 1, zw))

        @pl.when(is_top)
        def _():
            @pl.loop(1, nz)
            def _(k):
                act(fold_copy(p, z, (z + k) % nz))

    def halo_arrive(p):
        col_copy(p, 0, m, ze).wait_recv()
        col_copy(p, 3, m, zw).wait_recv()

        @pl.when(has_s)
        def _():
            row_copy(p, 0, m, ze).wait_recv()
            col_copy(p, 1, m, ze).wait_recv()
            col_copy(p, 4, m, zw).wait_recv()

        @pl.when(has_n)
        def _():
            row_copy(p, 1, m, ze).wait_recv()
            col_copy(p, 2, m, ze).wait_recv()
            col_copy(p, 5, m, zw).wait_recv()

        @pl.when(is_top)
        def _():
            fold_all[p, z, :, :] = row_send[p, 0, :, :]

            @pl.loop(1, nz)
            def _(k):
                fold_copy(p, (z + nz - k) % nz, ze).wait_recv()

    spot = lax.broadcasted_iota(jnp.int32, (cols, ch), 0)

    def emit(row, wrow, erow, q, off):
        left = jnp.where(spot == 0, wrow, pltpu.roll(row, 1, 0))
        right = jnp.where(spot == cols - 1, erow, pltpu.roll(row, cols - 1, 0))
        q[pl.ds(off, cols), 0:ch] = left.astype(BF)
        q[pl.ds(off, cols), ch:2 * ch] = row.astype(BF)
        q[pl.ds(off, cols), 2 * ch:3 * ch] = right.astype(BF)

    def assemble(p, k, v, q, ql):
        mine = slice(k * rows, (k + 1) * rows)
        span = slice(k * cols, (k + 1) * cols)
        west[0:rows, :] = col_recv[p, 0, mine, :].astype(F32)
        east[0:rows, :] = col_recv[p, 3, mine, :].astype(F32)

        @pl.when(has_s)
        def _():
            south[...] = row_recv[p, 0, span, :].astype(F32)
            west[rows:rows + 1, :] = col_recv[p, 1, mine, :].astype(F32)[rows - 1:rows, :]
            east[rows:rows + 1, :] = col_recv[p, 4, mine, :].astype(F32)[rows - 1:rows, :]

        @pl.when(jnp.logical_not(has_s))
        def _():
            south[...] = jnp.zeros_like(south)
            west[rows:rows + 1, :] = jnp.zeros((1, ch), F32)
            east[rows:rows + 1, :] = jnp.zeros((1, ch), F32)

        @pl.when(has_n)
        def _():
            north[...] = row_recv[p, 1, span, :].astype(F32)
            west[rows + 1:rows + 2, :] = col_recv[p, 2, mine, :].astype(F32)[0:1, :]
            east[rows + 1:rows + 2, :] = col_recv[p, 5, mine, :].astype(F32)[0:1, :]

        @pl.when(is_top)
        def _():
            around = nz * cols
            extra = cols + 16
            first = partner_tab[0]
            at = lax.broadcasted_iota(jnp.int32, (extra, around), 0)
            column = z * cols + jnp.where(at < cols, at, jnp.where(at == cols, -1, cols))
            target = first - column
            target = jnp.where(target < 0, target + around, target)
            target = jnp.where(target >= around, target - around, target)
            source = lax.broadcasted_iota(jnp.int32, (extra, around), 1)
            pick = jnp.where(target == source, 1.0, 0.0).astype(BF)
            whole_row = fold_all[p, :, span, :].reshape(around, ch)
            folded = jnp.dot(pick, whole_row, preferred_element_type=F32)
            north[...] = folded[0:cols, :]
            west[rows + 1:rows + 2, :] = folded[cols:cols + 1, :]
            east[rows + 1:rows + 2, :] = folded[cols + 1:cols + 2, :]

        @pl.loop(0, rows, unroll=2)
        def _(y):
            off = pl.multiple_of(y * cols, cols)
            emit(
                v[pl.ds(off, cols), :], west[pl.ds(y, 1), :], east[pl.ds(y, 1), :],
                q, pl.multiple_of(off + cols, cols),
            )

        emit(south[...], west[rows:rows + 1, :], east[rows:rows + 1, :], q, 0)
        if ql is None:
            emit(north[...], west[rows + 1:rows + 2, :], east[rows + 1:rows + 2, :], q, cells + cols)
        else:
            emit(north[...], west[rows + 1:rows + 2, :], east[rows + 1:rows + 2, :], ql, 0)
            q[cells + cols:, :] = jnp.zeros((cols, 3 * ch), BF)

    chunk = 4 * cols

    def conv(q, w, finish):
        @pl.loop(0, cells // chunk)
        def _(i):
            off = pl.multiple_of(i * chunk, chunk)
            total = jnp.dot(q[pl.ds(off, chunk), :], w[0], preferred_element_type=F32)
            for a in (1, 2):
                at = pl.multiple_of(off + a * cols, cols)
                total += jnp.dot(q[pl.ds(at, chunk), :], w[a], preferred_element_type=F32)
            finish(pl.ds(off, chunk), total)

    def transpose_weights(w, wt, wl):
        @pl.loop(0, 3)
        def _(a):
            for b in range(3):
                turned = w[2 - a, (2 - b) * ch:(3 - b) * ch, :].astype(F32).T
                wt[a, b * ch:(b + 1) * ch, :] = turned.astype(BF)

        for b in range(3):
            @pl.when(is_top)
            def _():
                wl[b * ch:(b + 1) * ch, :] = wt[0, (2 - b) * ch:(3 - b) * ch, :]

            @pl.when(jnp.logical_not(is_top))
            def _():
                wl[b * ch:(b + 1) * ch, :] = wt[2, b * ch:(b + 1) * ch, :]

    def last_row(ql, wl, target):
        target[cells - cols:, :] += jnp.dot(ql[...], wl[...], preferred_element_type=F32)

    def gradient(g, a, q, e_turned):
        for b in range(3):
            part = jnp.dot(
                e_turned, q[a * cols:a * cols + cells, b * ch:(b + 1) * ch],
                preferred_element_type=F32,
            )
            acc[g, (3 * a + b) * ch:(3 * a + b + 1) * ch, :] = part.T

    def loop_rows(count, body):
        piece = next(size for size in (192, 96, 48, 16) if count % size == 0)

        @pl.loop(0, count // piece)
        def _(i):
            body(i * piece, piece)

    def reduce_all(g, a):
        lane = 3 * g + a
        plan = plans[a]
        low = 3 * a * ch
        place = 0
        place_wide = 0
        waits = []
        gathers = []
        for step, (axis, bit, size, halve, wide) in enumerate(plan):
            mine, other = partner_of(axis, bit)
            keep = low + mine * size if halve else low
            give = low + (1 - mine) * size if halve else low
            if halve:
                gathers.append((step, axis, bit, size, low))

            def fill(off, piece, give=give, place=place):
                ar_send[lane, pl.ds(place + pl.multiple_of(off, 16), piece), :] = acc[
                    g, pl.ds(pl.multiple_of(give + off, 16), piece), :
                ].astype(BF)

            if wide:
                source = acc.at[g, pl.ds(pl.multiple_of(give, 16), size)]
                landing, start = ar_wide, place_wide
                place_wide += size
            else:
                loop_rows(size, fill)
                source = ar_send.at[lane, pl.ds(place, size)]
                landing, start = ar_recv, place
            copy = copy_to(
                source, landing.at[lane, pl.ds(start, size)],
                ar_ss.at[lane, step], ar_rs.at[lane, step], other["merid"], other["zonal"],
            )
            copy.start()
            yield
            copy.wait_recv()
            if wide and not halve:
                copy.wait_send()
            else:
                waits.append(copy)

            def add(
                off, piece, keep=keep, place=place, rounded=not (halve or wide),
                landing=landing, start=start,
            ):
                at = pl.ds(pl.multiple_of(keep + off, 16), piece)
                here = pl.ds(start + pl.multiple_of(off, 16), piece)
                own = ar_send[lane, here, :].astype(F32) if rounded else acc[g, at, :]
                acc[g, at, :] = own + landing[lane, here, :].astype(F32)

            loop_rows(size, add)
            if not wide:
                place += size
            low = keep
        final = plan[-1][2]

        def settle(off, piece, low=low):
            at = pl.ds(pl.multiple_of(low + off, 16), piece)
            sums[g, at, :] = acc[g, at, :].astype(BF)

        loop_rows(final, settle)
        size = final
        for step, axis, bit, size, base in reversed(gathers):
            mine, other = partner_of(axis, bit)
            at = pl.ds(pl.multiple_of(base + mine * size, 16), size)
            theirs = pl.ds(pl.multiple_of(base + (1 - mine) * size, 16), size)
            copy = copy_to(
                sums.at[g, at], sums.at[g, at], ag_ss.at[lane, step], ag_rs.at[lane, step],
                other["merid"], other["zonal"],
            )
            copy.start()
            waits.append(copy)
            yield
            copy_to(
                sums.at[g, theirs], sums.at[g, theirs], ag_ss.at[lane, step], ag_rs.at[lane, step],
                other["merid"], other["zonal"],
            ).wait_recv()
        for copy in waits:
            copy.wait_send()

    va[...] = field[...].astype(F32)
    channel = lax.broadcasted_iota(jnp.int32, (cols, ch), 1)
    level = channel
    for first in range(LEV, ch, LEV):
        level = level - jnp.where(channel >= first, LEV, 0)
    for y in range(rows):
        at = slice(y * cols, (y + 1) * cols)
        wet = jnp.where(level < depth[:, y:y + 1], 1.0, 0.0)
        masked = cotangent[at, :].astype(F32) * wet
        mask[at, :] = wet
        vb[at, :] = masked
        delta_in[at, :] = masked.astype(BF)
    prepare(0)
    count = (
        2 + len(plans[0]) + jnp.where(has_n, 3, 0) + jnp.where(has_s, 3, 0)
        + jnp.where(is_top, nz - 1, 0)
    )
    pl.semaphore_wait(barrier, count)
    halo(0, "start")
    transpose_weights(w_two, wt_two, wl_two)
    halo_arrive(0)
    assemble(0, 0, va, q_field, None)
    assemble(0, 1, vb, q_two, ql_two)

    def finish_one(at, total):
        x = total + b_one[...]
        keep = mask[at, :]
        square = x * x
        t = jnp.tanh(GELU_A * x * (1.0 + GELU_B * square))
        half = 0.5 * (1.0 + t)
        va[at, :] = (x * half * keep).astype(BF).astype(F32)
        slope = half + 0.5 * x * (1.0 - t * t) * (GELU_A * (1.0 + 3.0 * GELU_B * square))
        gp[at, :] = slope * keep

    conv(q_field, w_one, finish_one)

    def finish_hg(at, total):
        hg[at, :] = total

    conv(q_two, wt_two, finish_hg)
    last_row(ql_two, wl_two, hg)

    @pl.loop(0, rows)
    def _(y):
        at = pl.ds(pl.multiple_of(y * cols, cols), cols)
        vb[at, :] = (gp[at, :] * hg[at, :]).astype(BF).astype(F32)

    prepare(1)
    halo(1, "start")

    chains = []

    def advance():
        going = [next(chain, "end") != "end" for chain in chains]
        return any(going)

    def begin(g, a, q, e_turned):
        gradient(g, a, q, e_turned)
        chain = reduce_all(g, a)
        next(chain)
        chains.append(chain)

    turned = vb[...].T.astype(BF)
    for a in range(3):
        begin(0, a, q_field, turned)
    halo_arrive(1)
    assemble(1, 0, va, q_hidden, None)
    advance()
    turned = delta_in[...].astype(F32).T.astype(BF)
    for a in range(3):
        begin(1, a, q_hidden, turned)
    advance()

    assemble(1, 1, vb, q_one, ql_one)
    advance()

    def finish_out(at, total):
        full = field[at, :].astype(F32) + total + b_two[...]
        out[at, :] = (full * mask[at, :]).astype(BF)

    conv(q_hidden, w_two, finish_out)
    advance()
    transpose_weights(w_one, wt_one, wl_one)
    advance()
    conv(q_one, wt_one, finish_hg)
    last_row(ql_one, wl_one, hg)
    advance()

    @pl.loop(0, rows)
    def _(y):
        at = pl.ds(pl.multiple_of(y * cols, cols), cols)
        in_grad[at, :] = (delta_in[at, :].astype(F32) + hg[at, :]).astype(BF)

    while advance():
        pass
    halo(0, "wait_send")
    halo(1, "wait_send")


def shards(
    field, weight_one, bias_one, weight_two, bias_two, depth_levels, fold_partner, cotangent,
    nz, nm,
):
    rows, cols, ch = field.shape
    cells = rows * cols
    total = 9 * ch
    plans = plan_steps(total, nz, nm)
    sent = max(sum(step[2] for step in plan if not step[4]) for plan in plans)
    sent_wide = max(sum(step[2] for step in plan if step[4]) for plan in plans)
    steps = len(plans[0])
    vmem = pl.BlockSpec(memory_space=pltpu.VMEM)
    smem = pl.BlockSpec(memory_space=pltpu.SMEM)
    wide = 3 * ch
    dma = pltpu.SemaphoreType.DMA
    out, in_grad, sums = pl.pallas_call(
        functools.partial(kernel, nz, nm, rows, cols, plans),
        out_shape=(
            jax.ShapeDtypeStruct((cells, ch), BF),
            jax.ShapeDtypeStruct((cells, ch), BF),
            jax.ShapeDtypeStruct((2, total, ch), BF),
        ),
        in_specs=[vmem] * 7 + [smem],
        out_specs=(vmem, vmem, vmem),
        scratch_shapes=[
            pltpu.VMEM((cells, ch), F32), pltpu.VMEM((cells, ch), F32),
            pltpu.VMEM((cells, ch), F32), pltpu.VMEM((cells, ch), F32),
            pltpu.VMEM((cells, ch), F32), pltpu.VMEM((cells, ch), BF),
            pltpu.VMEM((cells + 2 * cols, wide), BF), pltpu.VMEM((cells + 2 * cols, wide), BF),
            pltpu.VMEM((cells + 2 * cols, wide), BF), pltpu.VMEM((cells + 2 * cols, wide), BF),
            pltpu.VMEM((cols, wide), BF), pltpu.VMEM((cols, wide), BF),
            pltpu.VMEM((3, wide, ch), BF), pltpu.VMEM((3, wide, ch), BF),
            pltpu.VMEM((wide, ch), BF), pltpu.VMEM((wide, ch), BF),
            pltpu.VMEM((rows + 8, ch), F32), pltpu.VMEM((rows + 8, ch), F32),
            pltpu.VMEM((cols, ch), F32), pltpu.VMEM((cols, ch), F32),
            pltpu.VMEM((rows, ch), F32),
            pltpu.VMEM((2, 2, 2 * cols, ch), BF), pltpu.VMEM((2, 2, 2 * rows, ch), BF),
            pltpu.VMEM((2, 2, 2 * cols, ch), BF), pltpu.VMEM((2, 6, 2 * rows, ch), BF),
            pltpu.VMEM((2, nz, 2 * cols, ch), BF),
            pltpu.VMEM((2, total, ch), F32),
            pltpu.VMEM((6, sent, ch), BF), pltpu.VMEM((6, sent, ch), BF),
            pltpu.VMEM((6, sent_wide, ch), F32),
            dma((2, 8)), dma((2, 8)), dma((2, nz)), dma((2, nz)),
            dma((6, steps)), dma((6, steps)), dma((6, steps)), dma((6, steps)),
        ],
        compiler_params=pltpu.CompilerParams(
            collective_id=0, has_side_effects=True, vmem_limit_bytes=58 * 1024 * 1024
        ),
    )(
        field.reshape(cells, ch), cotangent.reshape(cells, ch), depth_levels.T,
        weight_one.reshape(3, wide, ch), bias_one.reshape(1, ch),
        weight_two.reshape(3, wide, ch), bias_two.reshape(1, ch), fold_partner,
    )
    scale = 1.0 / math.sqrt(cells * nz * nm)
    grads = sums.astype(F32) * scale
    shape = weight_one.shape
    return (
        out.reshape(field.shape), in_grad.reshape(field.shape),
        grads[0].reshape(shape), grads[1].reshape(shape),
    )


def solution(mesh):
    placed = (
        P("merid", "zonal", None), P(), P(), P(), P(), P("merid", "zonal"), P(),
        P("merid", "zonal", None),
    )
    return jax.shard_map(
        functools.partial(shards, nz=mesh.shape["zonal"], nm=mesh.shape["merid"]),
        mesh=mesh,
        in_specs=placed,
        out_specs=(P("merid", "zonal", None), P("merid", "zonal", None), P(), P()),
        check_vma=False,
    )
```
